32 devices in a mesh: depth: 4 (over z), probe: 8 (over y, x, core).
Axes of the slice: x: 2, y: 2, z: 4, core: 2. Of those that a mesh axis runs over, the one named last changes fastest.
Arguments:
- residual: bfloat16 [32, 2, 256, 256], P('probe'), may hold values from -4 to 4
- saved_waves: bfloat16 [8, 32, 2, 256, 256], P('depth', 'probe'), may hold values from -4 to 4
- object_phase: float32 [8, 384, 384], P('depth'), may hold values from -3.140625 to 3.140625
- object_amp: float32 [8, 384, 384], P('depth'), may hold values from 0.25 to 1.75
- prop_phase: float32 [256, 256], replicated, may hold values from -3.140625 to 3.140625
- offsets: int32 [32, 2], P('probe'), may hold values from 0 to 128
Outputs:
- object_grad: float32 [8, 2, 384, 384], P('depth', None, 'probe')
- probe_grad: float32 [2, 256, 256], P(None, 'probe', 'depth')
The draws below stay inside these ranges and needn't reach their ends.
Inputs may be any that keep to these rules, and one draw needn't show every extreme that they name: `offsets`: every window lies inside the patch.
All inputs are finite; a program needn't handle non-finite values.
Results may differ from the reference program's by a relative error of at most 0.025.
The reference program's roundings to bfloat16 on the way (of `chi`) count: a program that leaves them out, or rounds other values in their place, can miss the bound.
Values may be sent and summed in bfloat16 or wider, within the bound.
A program may use at most 128 MiB of HBM per device.

```python
import math
import jax
import jax.numpy as jnp
from jax import lax

M = 256
PATCH = 384
SLICES = 8
POSITIONS = 32


def set_ends(values, key, least, high):
    dims = values.shape
    spot = [jax.random.randint(jax.random.fold_in(key, axis), (), 0, dims[axis]) for axis in range(len(dims))]
    values = values.at[tuple(spot)].set(least)
    longest = dims.index(max(dims))
    spot[longest] = (spot[longest] + 1) % dims[longest]
    return values.at[tuple(spot)].set(high)


def shard_levels(stream_key, extent, cuts, low, top_value):
    gain, own = 1.0, jax.random.fold_in(stream_key, 6)
    for axis_at, blocks in cuts:
        heights = jnp.exp(jax.random.uniform(jax.random.fold_in(own, axis_at), (blocks,), jnp.float32, low / len(cuts), top_value / len(cuts)))
        gain = gain * jnp.repeat(heights, extent[axis_at] // blocks).reshape([-1 if axis == axis_at else 1 for axis in range(len(extent))])
    return gain


def centred(key, dims, scale, reach, split=(), kind=jnp.bfloat16):
    values = jax.random.normal(key, dims, jnp.float32) * scale
    if len(split) > 0:
        values = shard_levels(key, dims, split, -0.22, 0.18) * values
    return jnp.clip(values, min=-reach, max=reach).astype(kind)


def setup_inputs(seed: int = 0) -> dict:
    arg_keys = jax.random.split(jax.random.key(seed), 7)
    residual = centred(arg_keys[0], (POSITIONS, 2, M, M), 0.25, 4.0, ((0, 8),))
    saved_waves = centred(arg_keys[1], (SLICES, POSITIONS, 2, M, M), 0.3, 4.0, ((0, 4), (1, 8)))
    object_phase = jnp.clip(jax.random.uniform(arg_keys[2], (SLICES, PATCH, PATCH), jnp.float32, -3.140625, 3.140625), -3.140625, 3.140625)
    object_amp = jnp.clip(1.0 + 0.15 * jax.random.normal(arg_keys[3], (SLICES, PATCH, PATCH), jnp.float32), 0.25, 1.75)
    prop_phase = jnp.clip(jax.random.uniform(arg_keys[4], (M, M), jnp.float32, -3.140625, 3.140625), -3.140625, 3.140625)
    offsets = set_ends(jax.random.randint(arg_keys[5], (POSITIONS, 2), 0, PATCH - M + 1), jax.random.fold_in(arg_keys[5], 1), 0, PATCH - M).astype(jnp.int32)
    return dict(residual=residual, saved_waves=saved_waves, object_phase=object_phase, object_amp=object_amp, prop_phase=prop_phase, offsets=offsets)


def tables(width):
    rows = lax.broadcasted_iota(jnp.int32, (width, width), 0)
    cols = lax.broadcasted_iota(jnp.int32, (width, width), 1)
    phase = 2.0 * math.pi / width * (rows * cols % width).astype(jnp.float32)
    factor = 1.0 / math.sqrt(width)
    return ((jnp.cos(phase) * factor).astype(jnp.bfloat16), (jnp.sin(phase) * factor).astype(jnp.bfloat16))

def left_apply(real_part, imag_part, waves):
    block = jnp.concatenate([jnp.concatenate([real_part, -imag_part], 1), jnp.concatenate([imag_part, real_part], 1)], 0)
    batch, _, width, _ = waves.shape
    flat = waves.reshape(batch, 2 * width, width)
    result = jnp.einsum('jk,bkl->bjl', block.astype(jnp.float32), flat.astype(jnp.float32), precision=lax.Precision.HIGHEST)
    return result.reshape(batch, 2, width, width)

def right_apply(real_part, imag_part, waves):
    batch, _, width, _ = waves.shape
    real_table = real_part.astype(jnp.float32)
    imag_table = imag_part.astype(jnp.float32)
    wave_real = waves[:, 0].reshape(batch * width, width).astype(jnp.float32)
    wave_imag = waves[:, 1].reshape(batch * width, width).astype(jnp.float32)
    high = lax.Precision.HIGHEST
    out_real = jnp.dot(wave_real, real_table, precision=high) - jnp.dot(wave_imag, imag_table, precision=high)
    out_imag = jnp.dot(wave_real, imag_table, precision=high) + jnp.dot(wave_imag, real_table, precision=high)
    return jnp.stack([out_real, out_imag], 1).reshape(batch, 2, width, width)

def back_propagate(chi, cosine, sine, kernel_cos, kernel_sin):
    first = left_apply(cosine, -sine, chi)
    spectrum = right_apply(cosine, -sine, first)
    spec_real = spectrum[:, 0]
    spec_imag = spectrum[:, 1]
    filtered = jnp.stack([kernel_cos * spec_real + kernel_sin * spec_imag, kernel_cos * spec_imag - kernel_sin * spec_real], 1)
    second = left_apply(cosine, sine, filtered)
    return right_apply(cosine, sine, second)

def reference(residual, saved_waves, object_phase, object_amp, prop_phase, offsets):
    width = residual.shape[-1]
    patch = object_phase.shape[-1]
    slice_count = object_phase.shape[0]
    cosine, sine = tables(width)
    kernel_cos = jnp.cos(prop_phase)
    kernel_sin = jnp.sin(prop_phase)
    trans_real = object_amp * jnp.cos(object_phase)
    trans_imag = object_amp * jnp.sin(object_phase)
    zero_index = jnp.zeros((), jnp.int32)

    def visit(carry, index):
        grads, probe_total = carry
        chi = lax.dynamic_index_in_dim(residual, index, 0, keepdims=True)
        row_start = offsets[index, 0].astype(jnp.int32)
        col_start = offsets[index, 1].astype(jnp.int32)
        for layer in range(slice_count - 1, -1, -1):
            arrived = back_propagate(chi, cosine, sine, kernel_cos, kernel_sin)[0]
            chi_real = arrived[0]
            chi_imag = arrived[1]
            wave = lax.dynamic_index_in_dim(saved_waves[layer], index, 0, keepdims=False).astype(jnp.float32)
            psi_real = wave[0]
            psi_imag = wave[1]
            term = jnp.stack([psi_real * chi_real + psi_imag * chi_imag, psi_real * chi_imag - psi_imag * chi_real])
            layer_grad = grads[layer]
            window = lax.dynamic_slice(layer_grad, (zero_index, row_start, col_start), (2, width, width))
            layer_grad = lax.dynamic_update_slice(layer_grad, window + term, (zero_index, row_start, col_start))
            grads = grads.at[layer].set(layer_grad)
            tr = lax.dynamic_slice(trans_real[layer], (row_start, col_start), (width, width))
            ti = lax.dynamic_slice(trans_imag[layer], (row_start, col_start), (width, width))
            chi = jnp.stack([tr * chi_real + ti * chi_imag, tr * chi_imag - ti * chi_real])[None].astype(jnp.bfloat16)
        probe_total = probe_total + chi[0].astype(jnp.float32)
        return ((grads, probe_total), None)
    start_grads = jnp.zeros((slice_count, 2, patch, patch), jnp.float32)
    start_probe = jnp.zeros((2, width, width), jnp.float32)
    indices = jnp.arange(residual.shape[0], dtype=jnp.int32)
    (grads, probe_total), _ = lax.scan(visit, (start_grads, start_probe), indices)
    return (grads, probe_total)
```

```python
import functools
import math

import jax
import jax.numpy as jnp
import ml_dtypes
import numpy as np
from jax import lax
from jax.experimental import pallas as pl
from jax.experimental.pallas import tpu as pltpu
from jax.sharding import PartitionSpec as P

LANES = 128
SUBLANES = 8
VMEM_BYTES = 56 * 1024 * 1024


def half_tables(width):
    half = width // 2
    at = np.arange(width)
    phase = 2.0 * math.pi / width * (np.outer(at, at) % width)
    cosine = np.cos(phase) / math.sqrt(width)
    sine = np.sin(phase) / math.sqrt(width)
    blocks = []
    for parity in (0, 1):
        c, s = cosine[:half, parity::2], sine[:half, parity::2]
        blocks.append(np.block([[c, s], [-s, c]]))
    for parity in (0, 1):
        c, s = cosine[:half, parity::2], sine[:half, parity::2]
        blocks.append(np.block([[c, -s], [s, c]]))
    for parity in (0, 1):
        c, s = cosine[parity::2, :half], sine[parity::2, :half]
        blocks.append(np.block([[c, s], [-s, c]]))
    return np.stack(blocks).astype(np.float32).astype(ml_dtypes.bfloat16)


def order_table(width):
    order = np.concatenate([np.arange(0, width, 2), np.arange(1, width, 2)])
    table = np.zeros((width, width), np.float32)
    table[np.arange(width), order] = 1.0
    return table


def rows(*blocks):
    return jnp.concatenate(blocks, 0)


def cols(*blocks):
    return jnp.concatenate(blocks, 1)


def dot(a, b):
    return jnp.dot(a, b, preferred_element_type=jnp.float32)


def back_propagate(x_real, x_imag, tables, kernel_cos, kernel_sin):
    half = x_real.shape[0] // 2
    low = jnp.bfloat16
    spans = (slice(0, half), slice(half, 2 * half))
    even = dot(tables[0], rows(x_real[:half], x_imag[:half]))
    odd = dot(tables[1], rows(x_real[half:], x_imag[half:]))
    sums, gaps = [], []
    for part in (even + odd, even - odd):
        left, right = part[:, :half], part[:, half:]
        total, gap = (left + right).astype(low), (left - right).astype(low)
        sums.append(cols(total[:half], total[half:]))
        gaps.append(cols(gap[:half], gap[half:]))
    spec_even = dot(rows(*sums), tables[2])
    spec_odd = dot(rows(*gaps), tables[3])
    parts = []
    for parity in spans:
        z_real, z_imag = [], []
        for at, spec in zip(spans, (spec_even, spec_odd)):
            real, imag = spec[:half, parity], spec[half:, parity]
            kc, ks = kernel_cos[parity, at], kernel_sin[parity, at]
            z_real.append((kc * real + ks * imag).astype(low))
            z_imag.append((kc * imag - ks * real).astype(low))
        parts.append(rows(cols(*z_real), cols(*z_imag)))
    even, odd = dot(tables[2], parts[0]), dot(tables[3], parts[1])
    top, bottom = (even + odd).astype(low), (even - odd).astype(low)
    ends = []
    for at, span in enumerate(spans):
        block = rows(
            cols(top[:half, span], top[half:, span]),
            cols(bottom[:half, span], bottom[half:, span]),
        )
        ends.append(dot(block, tables[4 + at]))
    sides = ends[0] + ends[1], ends[0] - ends[1]
    return [[(side[:half, parity], side[half:, parity]) for side in sides] for parity in spans]


def tile_rows(block):
    return block.reshape(block.shape[0] // SUBLANES, SUBLANES, block.shape[1])


def rows_earlier(block, count):
    tiles = pltpu.roll(tile_rows(block), lax.rem(SUBLANES - count, SUBLANES), 1)
    near = lax.broadcasted_iota(jnp.int32, tiles[1:].shape, 1) < SUBLANES - count
    kept = jnp.where(near, tiles[:-1], tiles[1:])
    return kept.reshape(block.shape[0] - SUBLANES, block.shape[1])


def rows_later(block, count):
    tiles = pltpu.roll(tile_rows(block), count, 1)
    zero = jnp.zeros_like(tiles[:1])
    below, above = rows(tiles, zero), rows(zero, tiles)
    far = lax.broadcasted_iota(jnp.int32, below.shape, 1) >= count
    return jnp.where(far, below, above).reshape(block.shape[0] + SUBLANES, block.shape[1])


def adjoint_kernel(
    place_ref,
    offsets_ref,
    residual_ref,
    waves_ref,
    trans_ref,
    phase_ref,
    tables_ref,
    order_ref,
    grads_ref,
    probe_ref,
    chi,
    layer_trans,
    kernel_cos,
    kernel_sin,
    totals,
    woven,
):
    positions, _, width, _ = residual_ref.shape
    sections, bands, own, _, band_rows, patch = trans_ref.shape
    section = place_ref[0]
    order = order_ref[...]
    exact = functools.partial(
        lax.dot_general, precision=lax.Precision.HIGHEST, preferred_element_type=jnp.float32
    )
    ordered = exact(order, phase_ref[...], (((1,), (0,)), ((), ())))
    ordered = exact(ordered, order, (((1,), (1,)), ((), ())))
    kernel_cos[...] = jnp.cos(ordered)
    kernel_sin[...] = jnp.sin(ordered)
    totals[...] = jnp.zeros_like(totals)
    half = width // 2
    split = order.astype(jnp.bfloat16)
    for position in range(positions):
        for part in (0, 1):
            chi[position, part] = dot(split, residual_ref[position, part]).astype(chi.dtype)
    lane = lax.broadcasted_iota(jnp.int32, (half + SUBLANES, LANES), 1)
    spans = (slice(0, LANES), slice(LANES, 2 * LANES), slice(2 * LANES, 3 * LANES))

    def layer_step(at_section, layer, deposit):
        for part in (0, 1):
            for band in range(bands):
                block = trans_ref[at_section, band, layer, part].astype(jnp.float32)
                count = band_rows // 2
                for parity in (0, 1):
                    layer_trans[part, parity, pl.ds(band * count, count), :] = block[
                        parity * count : (parity + 1) * count
                    ]
        for position in range(positions):
            row_at = offsets_ref[position, 0]
            col_at = offsets_ref[position, 1]
            into = lax.rem(LANES - col_at, LANES)
            outof = lax.rem(col_at, LANES)
            behind = lane < LANES - col_at
            ahead = lane >= col_at
            tables = [tables_ref[k] for k in range(6)]
            q = back_propagate(
                chi[position, 0], chi[position, 1], tables, kernel_cos, kernel_sin
            )
            if deposit:
                psi = [dot(split, waves_ref[layer, position, part]) for part in (0, 1)]
            for parity in (0, 1):
                first = (row_at + parity) // 2
                plane = lax.rem(row_at + parity, 2)
                rest = lax.rem(first, SUBLANES)
                window = pl.ds(pl.multiple_of(first - rest, SUBLANES), half + SUBLANES)
                own_rows = slice(parity * half, (parity + 1) * half)
                if deposit:
                    terms = ([], [])
                    for at in (0, 1):
                        real, imag = q[parity][at]
                        psi_real, psi_imag = (plane_of[own_rows, spans[at]] for plane_of in psi)
                        pair = psi_real * real + psi_imag * imag, psi_real * imag - psi_imag * real
                        for part in (0, 1):
                            terms[part].append(
                                pltpu.roll(rows_later(pair[part], rest), outof, 1)
                            )
                    for part in (0, 1):
                        left, right = terms[part]
                        shifted = (
                            jnp.where(ahead, left, 0.0),
                            jnp.where(ahead, right, left),
                            jnp.where(ahead, 0.0, right),
                        )
                        for at in range(3):
                            totals[layer, part, plane, window, spans[at]] += shifted[at]
                trans = []
                for part in (0, 1):
                    tiles = [
                        pltpu.roll(layer_trans[part, plane, window, spans[at]], into, 1)
                        for at in range(3)
                    ]
                    trans.append(
                        [
                            rows_earlier(jnp.where(behind, tiles[at], tiles[at + 1]), rest)
                            for at in (0, 1)
                        ]
                    )
                for at in (0, 1):
                    real, imag = q[parity][at]
                    tr, ti = trans[0][at], trans[1][at]
                    chi[position, 0, own_rows, spans[at]] = (tr * real + ti * imag).astype(chi.dtype)
                    chi[position, 1, own_rows, spans[at]] = (tr * imag - ti * real).astype(chi.dtype)

    def deeper(step, carry):
        index = sections * own - 1 - step
        layer_step(index // own, lax.rem(index, own), False)
        return carry

    lax.fori_loop(0, (sections - 1 - section) * own, deeper, 0)

    def mine(step, carry):
        layer_step(section, own - 1 - step, True)
        return carry

    lax.fori_loop(0, own, mine, 0)
    for part in (0, 1):
        for layer in range(own):
            for at, span in enumerate(spans):
                for parity in (0, 1):
                    woven[at, pl.ds(parity, patch // 2, 2), :] = totals[
                        layer, part, parity, : patch // 2, span
                    ]
                grads_ref[layer, part, :, span] = woven[at]
        for parity in (0, 1):
            own_rows = slice(parity * half, (parity + 1) * half)
            total = chi[0, part, own_rows].astype(jnp.float32)
            for position in range(1, positions):
                total = total + chi[position, part, own_rows].astype(jnp.float32)
            total = jnp.where(section == 0, total, 0.0)
            for at, span in enumerate(spans[:2]):
                woven[at, pl.ds(parity, half, 2), :] = total[:, span]
        for at, span in enumerate(spans[:2]):
            probe_ref[part, :, span] = woven[at, :width]


def shards(residual, saved_waves, object_phase, object_amp, prop_phase, offsets):
    positions, _, width, _ = residual.shape
    own, patch, _ = object_phase.shape
    sections = lax.axis_size("depth")
    bands = lax.axis_size("probe")
    section = lax.axis_index("depth")
    band_rows = patch // bands
    assert width == 2 * LANES and patch == 3 * LANES

    start = lax.axis_index("probe") * band_rows
    phase = lax.dynamic_slice_in_dim(object_phase, start, band_rows, 1)
    amp = lax.dynamic_slice_in_dim(object_amp, start, band_rows, 1)
    share = jnp.stack([amp * jnp.cos(phase), amp * jnp.sin(phase)], 1).astype(jnp.bfloat16)
    share = share.reshape(own, 2, band_rows // 2, 2, patch).swapaxes(2, 3)
    share = share.reshape(own, 2, band_rows, patch)
    trans = lax.all_gather(share, ("depth", "probe"))
    trans = trans.reshape((sections, bands) + share.shape)

    vmem = pl.BlockSpec(memory_space=pltpu.VMEM)
    smem = pl.BlockSpec(memory_space=pltpu.SMEM)
    grads, probe_sum = pl.pallas_call(
        adjoint_kernel,
        out_shape=(
            jax.ShapeDtypeStruct((own, 2, patch, patch), jnp.float32),
            jax.ShapeDtypeStruct((2, width, width), jnp.float32),
        ),
        in_specs=[smem, smem] + [vmem] * 6,
        out_specs=(vmem, vmem),
        scratch_shapes=[
            pltpu.VMEM(residual.shape, jnp.bfloat16),
            pltpu.VMEM((2, 2, patch // 2 + SUBLANES, patch), jnp.float32),
            pltpu.VMEM((width, width), jnp.float32),
            pltpu.VMEM((width, width), jnp.float32),
            pltpu.VMEM((own, 2, 2, patch // 2 + SUBLANES, patch), jnp.float32),
            pltpu.VMEM((3, patch, LANES), jnp.float32),
        ],
        compiler_params=pltpu.CompilerParams(vmem_limit_bytes=VMEM_BYTES),
        name="adjoint",
    )(
        section.astype(jnp.int32)[None],
        offsets,
        residual,
        saved_waves,
        trans,
        prop_phase,
        jnp.asarray(half_tables(width)),
        jnp.asarray(order_table(width)),
    )
    object_grad = lax.psum_scatter(grads, "probe", scatter_dimension=2, tiled=True)
    rows_each, cols_each = width // bands, width // sections
    blocks = probe_sum.reshape(2, bands, rows_each, sections, cols_each)
    blocks = blocks.transpose(1, 3, 0, 2, 4).reshape(bands * sections, 2, rows_each, cols_each)
    probe_grad = lax.psum_scatter(blocks, ("probe", "depth"), scatter_dimension=0, tiled=False)
    return (object_grad, probe_grad)


def solution(mesh):
    return jax.shard_map(
        shards,
        mesh=mesh,
        in_specs=(
            P("probe", None, None, None),
            P("depth", "probe", None, None, None),
            P("depth", None, None),
            P("depth", None, None),
            P(),
            P("probe", None),
        ),
        out_specs=(P("depth", None, "probe", None), P(None, "probe", "depth")),
        check_vma=False,
    )
```

```python
import functools
import math

import jax
import jax.numpy as jnp
import ml_dtypes
import numpy as np
from jax import lax
from jax.experimental import pallas as pl
from jax.experimental.pallas import tpu as pltpu
from jax.sharding import PartitionSpec as P

LANES = 128
SUBLANES = 8
VMEM_BYTES = 56 * 1024 * 1024


def half_tables(width):
    half = width // 2
    at = np.arange(width)
    phase = 2.0 * math.pi / width * (np.outer(at, at) % width)
    cosine = np.cos(phase) / math.sqrt(width)
    sine = np.sin(phase) / math.sqrt(width)
    blocks = []
    for parity in (0, 1):
        c, s = cosine[:half, parity::2], sine[:half, parity::2]
        blocks.append(np.block([[c, s], [-s, c]]))
    for parity in (0, 1):
        c, s = cosine[:half, parity::2], sine[:half, parity::2]
        blocks.append(np.block([[c, -s], [s, c]]))
    for parity in (0, 1):
        c, s = cosine[parity::2, :half], sine[parity::2, :half]
        blocks.append(np.block([[c, s], [-s, c]]))
    return np.stack(blocks).astype(np.float32).astype(ml_dtypes.bfloat16)


def order_table(width):
    order = np.concatenate([np.arange(0, width, 2), np.arange(1, width, 2)])
    table = np.zeros((width, width), np.float32)
    table[np.arange(width), order] = 1.0
    return table


def rows(*blocks):
    return jnp.concatenate(blocks, 0)


def cols(*blocks):
    return jnp.concatenate(blocks, 1)


def dot(a, b):
    return jnp.dot(a, b, preferred_element_type=jnp.float32)


def back_propagate(x_real, x_imag, tables, kernel_cos, kernel_sin):
    half = x_real.shape[0] // 2
    low = jnp.bfloat16
    spans = (slice(0, half), slice(half, 2 * half))
    even = dot(tables[0], rows(x_real[:half], x_imag[:half]))
    odd = dot(tables[1], rows(x_real[half:], x_imag[half:]))
    sums, gaps = [], []
    for part in (even + odd, even - odd):
        left, right = part[:, :half], part[:, half:]
        total, gap = (left + right).astype(low), (left - right).astype(low)
        sums.append(cols(total[:half], total[half:]))
        gaps.append(cols(gap[:half], gap[half:]))
    spec_even = dot(rows(*sums), tables[2])
    spec_odd = dot(rows(*gaps), tables[3])
    parts = []
    for parity in spans:
        z_real, z_imag = [], []
        for at, spec in zip(spans, (spec_even, spec_odd)):
            real, imag = spec[:half, parity], spec[half:, parity]
            kc, ks = kernel_cos[parity, at], kernel_sin[parity, at]
            z_real.append((kc * real + ks * imag).astype(low))
            z_imag.append((kc * imag - ks * real).astype(low))
        parts.append(rows(cols(*z_real), cols(*z_imag)))
    even, odd = dot(tables[2], parts[0]), dot(tables[3], parts[1])
    top, bottom = (even + odd).astype(low), (even - odd).astype(low)
    ends = []
    for at, span in enumerate(spans):
        block = rows(
            cols(top[:half, span], top[half:, span]),
            cols(bottom[:half, span], bottom[half:, span]),
        )
        ends.append(dot(block, tables[4 + at]))
    sides = ends[0] + ends[1], ends[0] - ends[1]
    return [[(side[:half, parity], side[half:, parity]) for side in sides] for parity in spans]


def tile_rows(block):
    return block.reshape(block.shape[0] // SUBLANES, SUBLANES, block.shape[1])


def rows_earlier(block, count):
    tiles = pltpu.roll(tile_rows(block), lax.rem(SUBLANES - count, SUBLANES), 1)
    near = lax.broadcasted_iota(jnp.int32, tiles[1:].shape, 1) < SUBLANES - count
    kept = jnp.where(near, tiles[:-1], tiles[1:])
    return kept.reshape(block.shape[0] - SUBLANES, block.shape[1])


def rows_later(block, count):
    tiles = pltpu.roll(tile_rows(block), count, 1)
    zero = jnp.zeros_like(tiles[:1])
    below, above = rows(tiles, zero), rows(zero, tiles)
    far = lax.broadcasted_iota(jnp.int32, below.shape, 1) >= count
    return jnp.where(far, below, above).reshape(block.shape[0] + SUBLANES, block.shape[1])


def adjoint_kernel(
    place_ref,
    offsets_ref,
    residual_ref,
    waves_ref,
    trans_ref,
    phase_ref,
    tables_ref,
    order_ref,
    grads_ref,
    probe_ref,
    chi,
    layer_trans,
    kernel_cos,
    kernel_sin,
    totals,
    woven,
):
    positions, _, width, _ = residual_ref.shape
    sections, bands, own, _, band_rows, patch = trans_ref.shape
    section = place_ref[0]
    order = order_ref[...]
    exact = functools.partial(
        lax.dot_general, precision=lax.Precision.HIGHEST, preferred_element_type=jnp.float32
    )
    ordered = exact(order, phase_ref[...], (((1,), (0,)), ((), ())))
    ordered = exact(ordered, order, (((1,), (1,)), ((), ())))
    kernel_cos[...] = jnp.cos(ordered)
    kernel_sin[...] = jnp.sin(ordered)
    totals[...] = jnp.zeros_like(totals)
    half = width // 2
    split = order.astype(jnp.bfloat16)
    for position in range(positions):
        for part in (0, 1):
            chi[position, part] = dot(split, residual_ref[position, part]).astype(chi.dtype)
    lane = lax.broadcasted_iota(jnp.int32, (half + SUBLANES, LANES), 1)
    spans = (slice(0, LANES), slice(LANES, 2 * LANES), slice(2 * LANES, 3 * LANES))

    def layer_step(at_section, layer, deposit):
        for part in (0, 1):
            for band in range(bands):
                block = trans_ref[at_section, band, layer, part].astype(jnp.float32)
                count = band_rows // 2
                for parity in (0, 1):
                    layer_trans[part, parity, pl.ds(band * count, count), :] = block[
                        parity * count : (parity + 1) * count
                    ]
        for position in range(positions):
            row_at = offsets_ref[position, 0]
            col_at = offsets_ref[position, 1]
            into = lax.rem(LANES - col_at, LANES)
            outof = lax.rem(col_at, LANES)
            behind = lane < LANES - col_at
            ahead = lane >= col_at
            tables = [tables_ref[k] for k in range(6)]
            q = back_propagate(
                chi[position, 0], chi[position, 1], tables, kernel_cos, kernel_sin
            )
            if deposit:
                psi = [dot(split, waves_ref[layer, position, part]) for part in (0, 1)]
            for parity in (0, 1):
                first = (row_at + parity) // 2
                plane = lax.rem(row_at + parity, 2)
                rest = lax.rem(first, SUBLANES)
                window = pl.ds(pl.multiple_of(first - rest, SUBLANES), half + SUBLANES)
                own_rows = slice(parity * half, (parity + 1) * half)
                if deposit:
                    terms = ([], [])
                    for at in (0, 1):
                        real, imag = q[parity][at]
                        psi_real, psi_imag = (plane_of[own_rows, spans[at]] for plane_of in psi)
                        pair = psi_real * real + psi_imag * imag, psi_real * imag - psi_imag * real
                        for part in (0, 1):
                            terms[part].append(
                                pltpu.roll(rows_later(pair[part], rest), outof, 1)
                            )
                    for part in (0, 1):
                        left, right = terms[part]
                        shifted = (
                            jnp.where(ahead, left, 0.0),
                            jnp.where(ahead, right, left),
                            jnp.where(ahead, 0.0, right),
                        )
                        for at in range(3):
                            totals[layer, part, plane, window, spans[at]] += shifted[at]
                trans = []
                for part in (0, 1):
                    tiles = [
                        pltpu.roll(layer_trans[part, plane, window, spans[at]], into, 1)
                        for at in range(3)
                    ]
                    trans.append(
                        [
                            rows_earlier(jnp.where(behind, tiles[at], tiles[at + 1]), rest)
                            for at in (0, 1)
                        ]
                    )
                for at in (0, 1):
                    real, imag = q[parity][at]
                    tr, ti = trans[0][at], trans[1][at]
                    chi[position, 0, own_rows, spans[at]] = (tr * real + ti * imag).astype(chi.dtype)
                    chi[position, 1, own_rows, spans[at]] = (tr * imag - ti * real).astype(chi.dtype)

    def deeper(step, carry):
        index = sections * own - 1 - step
        layer_step(index // own, lax.rem(index, own), False)
        return carry

    lax.fori_loop(0, (sections - 1 - section) * own, deeper, 0)

    def mine(step, carry):
        layer_step(section, own - 1 - step, True)
        return carry

    lax.fori_loop(0, own, mine, 0)
    for part in (0, 1):
        for layer in range(own):
            for at, span in enumerate(spans):
                for parity in (0, 1):
                    woven[at, pl.ds(parity, patch // 2, 2), :] = totals[
                        layer, part, parity, : patch // 2, span
                    ]
                for band in range(bands):
                    grads_ref[band, layer, part, :, span] = woven[
                        at, band * band_rows : (band + 1) * band_rows
                    ].astype(grads_ref.dtype)
        for parity in (0, 1):
            own_rows = slice(parity * half, (parity + 1) * half)
            total = chi[0, part, own_rows].astype(jnp.float32)
            for position in range(1, positions):
                total = total + chi[position, part, own_rows].astype(jnp.float32)
            for at, span in enumerate(spans[:2]):
                woven[at, pl.ds(parity, half, 2), :] = total[:, span]
        for at, span in enumerate(spans[:2]):
            for band in range(bands):
                count = width // bands
                probe_ref[band, part, :, span] = woven[
                    at, band * count : (band + 1) * count
                ].astype(probe_ref.dtype)


MESH = pl.DeviceIdType.MESH


def partners(section, band, sections, bands):
    chips = bands // 2
    chip, core = band // 2, band % 2
    found = [(section, 2 * chip + 1 - core)]
    found += [(section, 2 * ((chip + j) % chips) + core) for j in range(1, chips)]
    found += [((section + j) % sections, band) for j in range(1, sections)]
    return found


def meet(section, band, sections, bands):
    barrier = pltpu.get_barrier_semaphore()
    others = partners(section, band, sections, bands)
    for other in others:
        pl.semaphore_signal(barrier, inc=1, device_id=other, device_id_type=MESH)
    pl.semaphore_wait(barrier, len(others))


def gather_kernel(
    sections,
    bands,
    share_ref,
    trans_ref,
    local_sem,
    down_send,
    down_recv,
    plane_send,
    plane_recv,
    pair_send,
    pair_recv,
):
    section, band = lax.axis_index("depth"), lax.axis_index("probe")
    chips = bands // 2
    chip, core = band // 2, band % 2
    meet(section, band, sections, bands)

    def send(source, slot, to, send_sem, recv_sem):
        return pltpu.make_async_remote_copy(
            src_ref=source,
            dst_ref=trans_ref.at[slot],
            send_sem=send_sem,
            recv_sem=recv_sem,
            device_id=to,
            device_id_type=MESH,
        )

    def down(target, origin):
        return send(
            share_ref, (origin, band), (target, band), down_send.at[target], down_recv.at[origin]
        )

    def across(origin, j, source):
        return send(
            source,
            (origin, band),
            (section, 2 * ((chip + j) % chips) + core),
            plane_send.at[origin, j],
            plane_recv.at[origin, j],
        )

    def to_pair(origin, j, source):
        slot = (origin, 2 * ((chip + chips - j) % chips) + core)
        return send(
            source if j == 0 else trans_ref.at[slot],
            slot,
            (section, 2 * chip + 1 - core),
            pair_send.at[origin, j],
            pair_recv.at[origin, j],
        )

    for target in range(sections - 1):

        @pl.when(section > target)
        def _(target=target):
            down(target, section).start()

    own_copy = pltpu.make_async_copy(share_ref, trans_ref.at[section, band], local_sem)
    own_copy.start()
    for j in range(1, chips):
        across(section, j, share_ref).start()
    to_pair(section, 0, share_ref).start()
    for origin in range(1, sections):

        @pl.when(section < origin)
        def _(origin=origin):
            down(0, origin).wait_recv()
            held = trans_ref.at[origin, band]
            for j in range(1, chips):
                across(origin, j, held).start()
            to_pair(origin, 0, held).start()

    for origin in range(sections):

        @pl.when(section <= origin)
        def _(origin=origin):
            for j in range(1, chips):
                across(origin, j, share_ref).wait_recv()
                to_pair(origin, j, None).start()

    for origin in range(sections):

        @pl.when(section <= origin)
        def _(origin=origin):
            for j in range(chips):
                to_pair(origin, j, share_ref).wait()
                if j:
                    across(origin, j, share_ref).wait_send()

    for target in range(sections - 1):

        @pl.when(section > target)
        def _(target=target):
            down(target, section).wait_send()

    own_copy.wait()


def scatter_kernel(
    sections,
    bands,
    grads_ref,
    probe_ref,
    object_out,
    probe_out,
    pair_g,
    sum_g,
    in_g,
    pair_p,
    sum_p,
    in_p,
    pieces,
    arrived,
    pair_send,
    pair_recv,
    plane_send,
    plane_recv,
    column_send,
    column_recv,
):
    section, band = lax.axis_index("depth"), lax.axis_index("probe")
    chips = bands // 2
    chip, core = band // 2, band % 2
    wide = jnp.float32
    meet(section, band, sections, bands)
    fields = ((probe_ref, pair_p, sum_p, in_p), (grads_ref, pair_g, sum_g, in_g))

    def chip_at(j):
        return (chip + j) % chips

    def to_pair(field, j):
        source, pair, _, _ = fields[field]
        return pltpu.make_async_remote_copy(
            src_ref=source.at[2 * chip_at(j) + 1 - core],
            dst_ref=pair.at[j],
            send_sem=pair_send.at[field, j],
            recv_sem=pair_recv.at[field, j],
            device_id=(section, 2 * chip + 1 - core),
            device_id_type=MESH,
        )

    def across(field, j):
        _, _, sums, into = fields[field]
        return pltpu.make_async_remote_copy(
            src_ref=sums.at[j],
            dst_ref=into.at[j],
            send_sem=plane_send.at[field, j],
            recv_sem=plane_recv.at[field, j],
            device_id=(section, 2 * chip_at(j) + core),
            device_id_type=MESH,
        )

    def up(target):
        return pltpu.make_async_remote_copy(
            src_ref=pieces.at[target],
            dst_ref=arrived,
            send_sem=column_send.at[target],
            recv_sem=column_recv,
            device_id=(target, band),
            device_id_type=MESH,
        )

    order = list(range(1, chips)) + [0]

    def begin(field):
        for j in order:
            to_pair(field, j).start()

    def pass_on(field):
        source, pair, sums, _ = fields[field]
        for j in order:
            to_pair(field, j).wait()
            both = source[2 * chip_at(j) + core].astype(wide) + pair[j].astype(wide)
            if j == 0:
                return both
            sums[j] = both.astype(sums.dtype)
            across(field, j).start()

    def finish(field, both):
        _, _, _, into = fields[field]
        for j in range(1, chips):
            across(field, j).wait()
            both = both + into[j].astype(wide)
        return both

    @pl.when(section == 0)
    def _():
        begin(0)

    begin(1)

    @pl.when(section == 0)
    def _():
        total = finish(0, pass_on(0))
        each = total.shape[-1] // sections
        for target in range(sections):
            pieces[target] = total[:, :, target * each : (target + 1) * each]
        for target in range(1, sections):
            up(target).start()
        probe_out[...] = pieces[0]

    object_out[...] = pass_on(1)
    object_out[...] = finish(1, object_out[...])

    @pl.when(section == 0)
    def _():
        for target in range(1, sections):
            up(target).wait_send()

    @pl.when(section > 0)
    def _():
        up(1).wait_recv()
        probe_out[...] = arrived[...]


def shards(residual, saved_waves, object_phase, object_amp, prop_phase, offsets):
    positions, _, width, _ = residual.shape
    own, patch, _ = object_phase.shape
    sections = lax.axis_size("depth")
    bands = lax.axis_size("probe")
    section = lax.axis_index("depth")
    band_rows = patch // bands
    chips = bands // 2
    assert width == 2 * LANES and patch == 3 * LANES

    start = lax.axis_index("probe") * band_rows
    phase = lax.dynamic_slice_in_dim(object_phase, start, band_rows, 1)
    amp = lax.dynamic_slice_in_dim(object_amp, start, band_rows, 1)
    share = jnp.stack([amp * jnp.cos(phase), amp * jnp.sin(phase)], 1).astype(jnp.bfloat16)
    share = share.reshape(own, 2, band_rows // 2, 2, patch).swapaxes(2, 3)
    share = share.reshape(own, 2, band_rows, patch)

    vmem = pl.BlockSpec(memory_space=pltpu.VMEM)
    smem = pl.BlockSpec(memory_space=pltpu.SMEM)
    anywhere = pl.BlockSpec(memory_space=pl.ANY)
    dma = pltpu.SemaphoreType.DMA
    trans = pl.pallas_call(
        functools.partial(gather_kernel, sections, bands),
        out_shape=jax.ShapeDtypeStruct((sections, bands) + share.shape, jnp.bfloat16),
        in_specs=[anywhere],
        out_specs=anywhere,
        scratch_shapes=[
            dma,
            dma((sections,)),
            dma((sections,)),
            dma((sections, chips)),
            dma((sections, chips)),
            dma((sections, chips)),
            dma((sections, chips)),
        ],
        compiler_params=pltpu.CompilerParams(collective_id=0, has_side_effects=True),
        name="gather",
    )(share)

    rows_each, cols_each = width // bands, width // sections
    grads, probe_sum = pl.pallas_call(
        adjoint_kernel,
        out_shape=(
            jax.ShapeDtypeStruct((bands, own, 2, band_rows, patch), jnp.bfloat16),
            jax.ShapeDtypeStruct((bands, 2, rows_each, width), jnp.bfloat16),
        ),
        in_specs=[smem, smem] + [vmem] * 6,
        out_specs=(vmem, vmem),
        scratch_shapes=[
            pltpu.VMEM(residual.shape, jnp.bfloat16),
            pltpu.VMEM((2, 2, patch // 2 + SUBLANES, patch), jnp.float32),
            pltpu.VMEM((width, width), jnp.float32),
            pltpu.VMEM((width, width), jnp.float32),
            pltpu.VMEM((own, 2, 2, patch // 2 + SUBLANES, patch), jnp.float32),
            pltpu.VMEM((3, patch, LANES), jnp.float32),
        ],
        compiler_params=pltpu.CompilerParams(vmem_limit_bytes=VMEM_BYTES),
        name="adjoint",
    )(
        section.astype(jnp.int32)[None],
        offsets,
        residual,
        saved_waves,
        trans,
        prop_phase,
        jnp.asarray(half_tables(width)),
        jnp.asarray(order_table(width)),
    )
    block_g, block_p = (own, 2, band_rows, patch), (2, rows_each, width)
    low = jnp.bfloat16
    return pl.pallas_call(
        functools.partial(scatter_kernel, sections, bands),
        out_shape=(
            jax.ShapeDtypeStruct(block_g, jnp.float32),
            jax.ShapeDtypeStruct((2, rows_each, cols_each), jnp.float32),
        ),
        in_specs=[vmem, vmem],
        out_specs=(vmem, vmem),
        scratch_shapes=[pltpu.VMEM((chips,) + block_g, low)] * 3
        + [pltpu.VMEM((chips,) + block_p, low)] * 3
        + [
            pltpu.VMEM((sections, 2, rows_each, cols_each), jnp.float32),
            pltpu.VMEM((2, rows_each, cols_each), jnp.float32),
            dma((2, chips)),
            dma((2, chips)),
            dma((2, chips)),
            dma((2, chips)),
            dma((sections,)),
            dma,
        ],
        compiler_params=pltpu.CompilerParams(
            collective_id=1, has_side_effects=True, vmem_limit_bytes=VMEM_BYTES
        ),
        name="scatter",
    )(grads, probe_sum)


def solution(mesh):
    return jax.shard_map(
        shards,
        mesh=mesh,
        in_specs=(
            P("probe", None, None, None),
            P("depth", "probe", None, None, None),
            P("depth", None, None),
            P("depth", None, None),
            P(),
            P("probe", None),
        ),
        out_specs=(P("depth", None, "probe", None), P(None, "probe", "depth")),
        check_vma=False,
    )
```

```python
import functools
import math

import jax
import jax.numpy as jnp
import ml_dtypes
import numpy as np
from jax import lax
from jax.experimental import pallas as pl
from jax.experimental.pallas import tpu as pltpu
from jax.sharding import PartitionSpec as P

LANES = 128
SUBLANES = 8
VMEM_BYTES = 56 * 1024 * 1024


def half_tables(width):
    half = width // 2
    at = np.arange(width)
    phase = 2.0 * math.pi / width * (np.outer(at, at) % width)
    cosine = np.cos(phase) / math.sqrt(width)
    sine = np.sin(phase) / math.sqrt(width)
    blocks = []
    for parity in (0, 1):
        c, s = cosine[:half, parity::2], sine[:half, parity::2]
        blocks.append(np.block([[c, s], [-s, c]]))
    for parity in (0, 1):
        c, s = cosine[:half, parity::2], sine[:half, parity::2]
        blocks.append(np.block([[c, -s], [s, c]]))
    for parity in (0, 1):
        c, s = cosine[parity::2, :half], sine[parity::2, :half]
        blocks.append(np.block([[c, s], [-s, c]]))
    return np.stack(blocks).astype(np.float32).astype(ml_dtypes.bfloat16)


def order_table(width):
    order = np.concatenate([np.arange(0, width, 2), np.arange(1, width, 2)])
    table = np.zeros((width, width), np.float32)
    table[np.arange(width), order] = 1.0
    return table.astype(ml_dtypes.bfloat16)


def rows(*blocks):
    return jnp.concatenate(blocks, 0)


def cols(*blocks):
    return jnp.concatenate(blocks, 1)


def dot(a, b):
    return jnp.dot(a, b, preferred_element_type=jnp.float32)


def back_propagate(x_real, x_imag, tables, kernel_cos, kernel_sin):
    half = x_real.shape[0] // 2
    low = jnp.bfloat16
    spans = (slice(0, half), slice(half, 2 * half))
    even = dot(tables[0], rows(x_real[:half], x_imag[:half]))
    odd = dot(tables[1], rows(x_real[half:], x_imag[half:]))
    sums, gaps = [], []
    for part in (even + odd, even - odd):
        left, right = part[:, :half], part[:, half:]
        total, gap = (left + right).astype(low), (left - right).astype(low)
        sums.append(cols(total[:half], total[half:]))
        gaps.append(cols(gap[:half], gap[half:]))
    spec_even = dot(rows(*sums), tables[2])
    spec_odd = dot(rows(*gaps), tables[3])
    parts = []
    for parity in spans:
        z_real, z_imag = [], []
        for at, spec in zip(spans, (spec_even, spec_odd)):
            real, imag = spec[:half, parity], spec[half:, parity]
            kc, ks = kernel_cos[parity, at], kernel_sin[parity, at]
            z_real.append((kc * real + ks * imag).astype(low))
            z_imag.append((kc * imag - ks * real).astype(low))
        parts.append(rows(cols(*z_real), cols(*z_imag)))
    even, odd = dot(tables[2], parts[0]), dot(tables[3], parts[1])
    top, bottom = (even + odd).astype(low), (even - odd).astype(low)
    ends = []
    for at, span in enumerate(spans):
        block = rows(
            cols(top[:half, span], top[half:, span]),
            cols(bottom[:half, span], bottom[half:, span]),
        )
        ends.append(dot(block, tables[4 + at]))
    sides = ends[0] + ends[1], ends[0] - ends[1]
    return [[(side[:half, parity], side[half:, parity]) for side in sides] for parity in spans]


def tile_rows(block):
    return block.reshape(block.shape[0] // SUBLANES, SUBLANES, block.shape[1])


def rows_earlier(block, count):
    tiles = pltpu.roll(tile_rows(block), lax.rem(SUBLANES - count, SUBLANES), 1)
    near = lax.broadcasted_iota(jnp.int32, tiles[1:].shape, 1) < SUBLANES - count
    kept = jnp.where(near, tiles[:-1], tiles[1:])
    return kept.reshape(block.shape[0] - SUBLANES, block.shape[1])


def rows_later(block, count):
    tiles = pltpu.roll(tile_rows(block), count, 1)
    zero = jnp.zeros_like(tiles[:1])
    below, above = rows(tiles, zero), rows(zero, tiles)
    far = lax.broadcasted_iota(jnp.int32, below.shape, 1) >= count
    return jnp.where(far, below, above).reshape(block.shape[0] + SUBLANES, block.shape[1])


def cos_sin(angle):
    part = angle * 0.5
    square = part * part

    def series(first, count):
        terms = [(-1.0) ** k / math.factorial(2 * k + first) for k in range(count)]
        total = jnp.full_like(square, terms[-1])
        for term in terms[-2::-1]:
            total = total * square + term
        return total

    sine, cosine = part * series(1, 7), series(0, 8)
    return 1.0 - 2.0 * sine * sine, 2.0 * sine * cosine


def spans_of(count):
    return tuple(slice(k * LANES, (k + 1) * LANES) for k in range(count))


def layer_step(position, chi, tables_ref, kernel_cos, kernel_sin, trans_of, deposit=None):
    half = chi.shape[2] // 2
    spans = spans_of(2)
    tables = [tables_ref[k] for k in range(6)]
    q = back_propagate(chi[position, 0], chi[position, 1], tables, kernel_cos, kernel_sin)
    for parity in (0, 1):
        own_rows = slice(parity * half, (parity + 1) * half)
        if deposit is not None:
            deposit(q[parity], parity)
        trans = trans_of(parity)
        for at in (0, 1):
            real, imag = q[parity][at]
            tr, ti = trans[0][at], trans[1][at]
            chi[position, 0, own_rows, spans[at]] = (tr * real + ti * imag).astype(chi.dtype)
            chi[position, 1, own_rows, spans[at]] = (tr * imag - ti * real).astype(chi.dtype)


def own_kernel(
    offsets_ref,
    chi_ref,
    waves_ref,
    trans_ref,
    kernel_cos,
    kernel_sin,
    tables_ref,
    order_ref,
    grads_ref,
    probe_ref,
    chi,
    totals,
    woven,
):
    positions, _, width, _ = chi_ref.shape
    bands, own, _, band_rows, patch = grads_ref.shape
    half = width // 2
    split = order_ref[...]
    spans = spans_of(3)
    totals[...] = jnp.zeros_like(totals)
    chi[...] = chi_ref[...]

    def mine(step, carry):
        layer = own - 1 - step
        lane = lax.broadcasted_iota(jnp.int32, (half + SUBLANES, LANES), 1)
        for position in range(positions):
            psi = [dot(split, waves_ref[layer, position, part]) for part in (0, 1)]
            row_at = offsets_ref[position, 0]
            col_at = offsets_ref[position, 1]

            def place(parity, row_at=row_at):
                first = (row_at + parity) // 2
                plane = lax.rem(row_at + parity, 2)
                rest = lax.rem(first, SUBLANES)
                start = pl.multiple_of(first - rest, SUBLANES)
                return plane, pl.ds(start, half + SUBLANES), rest

            def trans_of(parity, place=place, col_at=col_at):
                plane, window, rest = place(parity)
                into = lax.rem(LANES - col_at, LANES)
                behind = lane < LANES - col_at
                trans = []
                for part in (0, 1):
                    tiles = [
                        pltpu.roll(trans_ref[layer, part, plane, window, spans[at]], into, 1)
                        for at in range(3)
                    ]
                    trans.append(
                        [
                            rows_earlier(jnp.where(behind, tiles[at], tiles[at + 1]), rest)
                            for at in (0, 1)
                        ]
                    )
                return trans

            def deposit(q, parity, psi=psi, place=place, col_at=col_at):
                plane, window, rest = place(parity)
                outof = lax.rem(col_at, LANES)
                ahead = lane >= col_at
                own_rows = slice(parity * half, (parity + 1) * half)
                terms = ([], [])
                for at in (0, 1):
                    real, imag = q[at]
                    psi_real, psi_imag = (plane_of[own_rows, spans[at]] for plane_of in psi)
                    pair = psi_real * real + psi_imag * imag, psi_real * imag - psi_imag * real
                    for part in (0, 1):
                        terms[part].append(pltpu.roll(rows_later(pair[part], rest), outof, 1))
                for part in (0, 1):
                    left, right = terms[part]
                    shifted = (
                        jnp.where(ahead, left, 0.0),
                        jnp.where(ahead, right, left),
                        jnp.where(ahead, 0.0, right),
                    )
                    for at in range(3):
                        totals[layer, part, plane, window, spans[at]] += shifted[at]

            layer_step(position, chi, tables_ref, kernel_cos, kernel_sin, trans_of, deposit)
        return carry

    lax.fori_loop(0, own, mine, 0)
    for part in (0, 1):
        for layer in range(own):
            for at, span in enumerate(spans):
                for parity in (0, 1):
                    woven[at, pl.ds(parity, patch // 2, 2), :] = totals[
                        layer, part, parity, : patch // 2, span
                    ]
                for band in range(bands):
                    grads_ref[band, layer, part, :, span] = woven[
                        at, band * band_rows : (band + 1) * band_rows
                    ].astype(grads_ref.dtype)
        for parity in (0, 1):
            own_rows = slice(parity * half, (parity + 1) * half)
            total = chi[0, part, own_rows].astype(jnp.float32)
            for position in range(1, positions):
                total = total + chi[position, part, own_rows].astype(jnp.float32)
            for at, span in enumerate(spans[:2]):
                woven[at, pl.ds(parity, half, 2), :] = total[:, span]
        for at, span in enumerate(spans[:2]):
            for band in range(bands):
                count = width // bands
                probe_ref[band, part, :, span] = woven[
                    at, band * count : (band + 1) * count
                ].astype(probe_ref.dtype)


MESH = pl.DeviceIdType.MESH


def partners(section, band, sections, bands):
    chips = bands // 2
    chip, core = band // 2, band % 2
    found = [(section, 2 * chip + 1 - core)]
    found += [(section, 2 * ((chip + j) % chips) + core) for j in range(1, chips)]
    found += [((section + j) % sections, band) for j in range(1, sections)]
    return found


def meet(section, band, sections, bands):
    barrier = pltpu.get_barrier_semaphore()
    others = partners(section, band, sections, bands)
    for other in others:
        pl.semaphore_signal(barrier, inc=1, device_id=other, device_id_type=MESH)
    pl.semaphore_wait(barrier, len(others))


def descend_kernel(
    sections,
    bands,
    offsets_ref,
    share_ref,
    residual_ref,
    phase_ref,
    amp_ref,
    prop_ref,
    tables_ref,
    order_ref,
    chi,
    own_trans,
    kernel_cos,
    kernel_sin,
    held,
    layer_wide,
    layer_trans,
    pick_rows,
    pick_cols,
    woven,
    down_send,
    down_recv,
    plane_send,
    plane_recv,
    pair_send,
    pair_recv,
):
    section, band = lax.axis_index("depth"), lax.axis_index("probe")
    chips = bands // 2
    chip, core = band // 2, band % 2
    positions = residual_ref.shape[0]
    own, _, band_rows, patch = share_ref.shape
    last = sections - 1
    meet(section, band, sections, bands)

    def send(source, slot, to, send_sem, recv_sem):
        return pltpu.make_async_remote_copy(
            src_ref=source,
            dst_ref=held.at[slot],
            send_sem=send_sem,
            recv_sem=recv_sem,
            device_id=to,
            device_id_type=MESH,
        )

    def down(target, origin):
        return send(
            share_ref, (origin, band), (target, band), down_send.at[target], down_recv.at[origin]
        )

    def across(origin, j):
        return send(
            held.at[origin, band],
            (origin, band),
            (section, 2 * ((chip + j) % chips) + core),
            plane_send.at[origin, j],
            plane_recv.at[origin, j],
        )

    def to_pair(origin, j):
        slot = (origin, 2 * ((chip + chips - j) % chips) + core)
        return send(
            held.at[slot],
            slot,
            (section, 2 * chip + 1 - core),
            pair_send.at[origin, j],
            pair_recv.at[origin, j],
        )

    def fan_out(origin):
        down(0, origin).wait_recv()
        for j in range(1, chips):
            across(origin, j).start()
        to_pair(origin, 0).start()

    def share_pair(origin):
        for j in range(1, chips):
            across(origin, j).wait_recv()
            to_pair(origin, j).start()

    def send_down():
        for target in range(last):

            @pl.when(section > target)
            def _(target=target):
                down(target, section).start()

    @pl.when(section == last)
    def _():
        send_down()

    split = order_ref[...]
    exact = functools.partial(
        lax.dot_general, precision=lax.Precision.HIGHEST, preferred_element_type=jnp.float32
    )
    order = split.astype(jnp.float32)
    ordered = exact(order, prop_ref[...], (((1,), (0,)), ((), ())))
    ordered = exact(ordered, order, (((1,), (1,)), ((), ())))
    kernel_cos[...], kernel_sin[...] = cos_sin(ordered)
    low = chi.dtype
    width = chi.shape[2]
    half = width // 2
    row = lax.broadcasted_iota(jnp.int32, (width, patch), 0)
    row_order = jnp.where(row < half, 2 * row, 2 * (row - half) + 1)
    row_from = lax.broadcasted_iota(jnp.int32, (width, patch), 1) - row_order
    col_from = lax.broadcasted_iota(jnp.int32, (patch, width), 0) - lax.broadcasted_iota(
        jnp.int32, (patch, width), 1
    )
    for position in range(positions):
        picked = jnp.where(row_from == offsets_ref[position, 0], 1.0, 0.0)
        pick_rows[position] = picked.astype(low)
        picked = jnp.where(col_from == offsets_ref[position, 1], 1.0, 0.0)
        pick_cols[position] = picked.astype(low)
        for part in (0, 1):
            chi[position, part] = dot(split, residual_ref[position, part]).astype(low)

    @pl.when(section < last)
    def _():
        fan_out(last)
        send_down()

    def own_layer(layer, carry):
        for at, span in enumerate(spans_of(3)):
            cosine, sine = cos_sin(phase_ref[layer, :, span])
            amp = amp_ref[layer, :, span]
            for part, field in enumerate((amp * cosine, amp * sine)):
                woven[part, at] = field
                for parity in (0, 1):
                    own_trans[layer, part, parity, : patch // 2, span] = woven[
                        part, at, pl.ds(parity, patch // 2, 2), :
                    ]
        for part in (0, 1):
            for parity in (0, 1):
                own_trans[layer, part, parity, patch // 2 :, :] = jnp.zeros(
                    (SUBLANES, patch), jnp.float32
                )
        return carry

    lax.fori_loop(0, own, own_layer, 0)
    def fan_rest(step, carry):
        fan_out(last - 1 - step)
        return carry

    @pl.when(section < last)
    def _():
        lax.fori_loop(0, last - 1 - section, fan_rest, 0)
        share_pair(last)

    def through(step, carry):
        origin = last - step
        for j in range(chips):
            to_pair(origin, j).wait_recv()

        def one_layer(step, carry):
            layer = own - 1 - step
            for part in (0, 1):
                for from_band in range(bands):
                    layer_wide[part, pl.ds(from_band * band_rows, band_rows), :] = held[
                        origin, from_band, layer, part
                    ].astype(jnp.float32)
                layer_trans[:, part * patch : (part + 1) * patch] = layer_wide[part].astype(low)
            for position in range(positions):
                across_rows = dot(pick_rows[position], layer_trans[...]).astype(low)
                window = [
                    dot(across_rows[:, part * patch : (part + 1) * patch], pick_cols[position])
                    for part in (0, 1)
                ]

                def trans_of(parity, window=window):
                    own_rows = slice(parity * half, (parity + 1) * half)
                    return [[plane[own_rows, span] for span in spans_of(2)] for plane in window]

                layer_step(position, chi, tables_ref, kernel_cos, kernel_sin, trans_of)

            @pl.when((step == 0) & (origin - 1 > section))
            def _():
                share_pair(origin - 1)

            return carry

        return lax.fori_loop(0, own, one_layer, carry)

    lax.fori_loop(0, last - section, through, 0)

    def settle(step, carry):
        origin = last - step
        for j in range(chips):
            to_pair(origin, j).wait_send()
            if j:
                across(origin, j).wait_send()
        return carry

    lax.fori_loop(0, last - section, settle, 0)
    for target in range(last):

        @pl.when(section > target)
        def _(target=target):
            down(target, section).wait_send()


def scatter_kernel(
    sections,
    bands,
    grads_ref,
    probe_ref,
    object_out,
    probe_out,
    pair_g,
    sum_g,
    in_g,
    pair_p,
    sum_p,
    in_p,
    pieces,
    arrived,
    pair_send,
    pair_recv,
    plane_send,
    plane_recv,
    column_send,
    column_recv,
):
    section, band = lax.axis_index("depth"), lax.axis_index("probe")
    chips = bands // 2
    chip, core = band // 2, band % 2
    wide = jnp.float32
    meet(section, band, sections, bands)
    fields = ((probe_ref, pair_p, sum_p, in_p), (grads_ref, pair_g, sum_g, in_g))

    def chip_at(j):
        return (chip + j) % chips

    def to_pair(field, j):
        source, pair, _, _ = fields[field]
        return pltpu.make_async_remote_copy(
            src_ref=source.at[2 * chip_at(j) + 1 - core],
            dst_ref=pair.at[j],
            send_sem=pair_send.at[field, j],
            recv_sem=pair_recv.at[field, j],
            device_id=(section, 2 * chip + 1 - core),
            device_id_type=MESH,
        )

    def across(field, j):
        _, _, sums, into = fields[field]
        return pltpu.make_async_remote_copy(
            src_ref=sums.at[j],
            dst_ref=into.at[j],
            send_sem=plane_send.at[field, j],
            recv_sem=plane_recv.at[field, j],
            device_id=(section, 2 * chip_at(j) + core),
            device_id_type=MESH,
        )

    def up(target):
        return pltpu.make_async_remote_copy(
            src_ref=pieces.at[target],
            dst_ref=arrived,
            send_sem=column_send.at[target],
            recv_sem=column_recv,
            device_id=(target, band),
            device_id_type=MESH,
        )

    order = list(range(1, chips)) + [0]

    def begin(field):
        for j in order:
            to_pair(field, j).start()

    def pass_on(field):
        source, pair, sums, _ = fields[field]
        for j in order:
            to_pair(field, j).wait()
            both = source[2 * chip_at(j) + core].astype(wide) + pair[j].astype(wide)
            if j == 0:
                return both
            sums[j] = both.astype(sums.dtype)
            across(field, j).start()

    def finish(field, both):
        _, _, _, into = fields[field]
        for j in range(1, chips):
            across(field, j).wait()
            both = both + into[j].astype(wide)
        return both

    @pl.when(section == 0)
    def _():
        begin(0)

    begin(1)

    @pl.when(section == 0)
    def _():
        total = finish(0, pass_on(0))
        each = total.shape[-1] // sections
        for target in range(sections):
            pieces[target] = total[:, :, target * each : (target + 1) * each]
        for target in range(1, sections):
            up(target).start()
        probe_out[...] = pieces[0]

    object_out[...] = pass_on(1)
    object_out[...] = finish(1, object_out[...])

    @pl.when(section == 0)
    def _():
        for target in range(1, sections):
            up(target).wait_send()

    @pl.when(section > 0)
    def _():
        up(1).wait_recv()
        probe_out[...] = arrived[...]


def shards(residual, saved_waves, object_phase, object_amp, prop_phase, offsets):
    positions, _, width, _ = residual.shape
    own, patch, _ = object_phase.shape
    sections = lax.axis_size("depth")
    bands = lax.axis_size("probe")
    band_rows = patch // bands
    chips = bands // 2
    assert width == 2 * LANES and patch == 3 * LANES

    start = lax.axis_index("probe") * band_rows
    phase = lax.dynamic_slice_in_dim(object_phase, start, band_rows, 1)
    amp = lax.dynamic_slice_in_dim(object_amp, start, band_rows, 1)
    share = jnp.stack([amp * jnp.cos(phase), amp * jnp.sin(phase)], 1).astype(jnp.bfloat16)

    vmem = pl.BlockSpec(memory_space=pltpu.VMEM)
    smem = pl.BlockSpec(memory_space=pltpu.SMEM)
    dma = pltpu.SemaphoreType.DMA
    tables = jnp.asarray(half_tables(width))
    order = jnp.asarray(order_table(width))
    split_trans = (own, 2, 2, patch // 2 + SUBLANES, patch)
    plane = jax.ShapeDtypeStruct((width, width), jnp.float32)
    chi, own_trans, kernel_cos, kernel_sin = pl.pallas_call(
        functools.partial(descend_kernel, sections, bands),
        out_shape=(
            jax.ShapeDtypeStruct(residual.shape, jnp.bfloat16),
            jax.ShapeDtypeStruct(split_trans, jnp.float32),
            plane,
            plane,
        ),
        in_specs=[smem] + [vmem] * 7,
        out_specs=(vmem,) * 4,
        scratch_shapes=[
            pltpu.VMEM((sections, bands) + share.shape, jnp.bfloat16),
            pltpu.VMEM((2, patch, patch), jnp.float32),
            pltpu.VMEM((patch, 2 * patch), jnp.bfloat16),
            pltpu.VMEM((positions, width, patch), jnp.bfloat16),
            pltpu.VMEM((positions, patch, width), jnp.bfloat16),
            pltpu.VMEM((2, 3, patch, LANES), jnp.float32),
            dma((sections,)),
            dma((sections,)),
            dma((sections, chips)),
            dma((sections, chips)),
            dma((sections, chips)),
            dma((sections, chips)),
        ],
        compiler_params=pltpu.CompilerParams(
            collective_id=0, has_side_effects=True, vmem_limit_bytes=VMEM_BYTES
        ),
        name="descend",
    )(offsets, share, residual, object_phase, object_amp, prop_phase, tables, order)

    rows_each, cols_each = width // bands, width // sections
    grads, probe_sum = pl.pallas_call(
        own_kernel,
        out_shape=(
            jax.ShapeDtypeStruct((bands, own, 2, band_rows, patch), jnp.bfloat16),
            jax.ShapeDtypeStruct((bands, 2, rows_each, width), jnp.bfloat16),
        ),
        in_specs=[smem] + [vmem] * 7,
        out_specs=(vmem, vmem),
        scratch_shapes=[
            pltpu.VMEM(residual.shape, jnp.bfloat16),
            pltpu.VMEM(split_trans, jnp.float32),
            pltpu.VMEM((3, patch, LANES), jnp.float32),
        ],
        compiler_params=pltpu.CompilerParams(vmem_limit_bytes=VMEM_BYTES),
        name="own",
    )(offsets, chi, saved_waves, own_trans, kernel_cos, kernel_sin, tables, order)
    block_g, block_p = (own, 2, band_rows, patch), (2, rows_each, width)
    low = jnp.bfloat16
    return pl.pallas_call(
        functools.partial(scatter_kernel, sections, bands),
        out_shape=(
            jax.ShapeDtypeStruct(block_g, jnp.float32),
            jax.ShapeDtypeStruct((2, rows_each, cols_each), jnp.float32),
        ),
        in_specs=[vmem, vmem],
        out_specs=(vmem, vmem),
        scratch_shapes=[pltpu.VMEM((chips,) + block_g, low)] * 3
        + [pltpu.VMEM((chips,) + block_p, low)] * 3
        + [
            pltpu.VMEM((sections, 2, rows_each, cols_each), jnp.float32),
            pltpu.VMEM((2, rows_each, cols_each), jnp.float32),
            dma((2, chips)),
            dma((2, chips)),
            dma((2, chips)),
            dma((2, chips)),
            dma((sections,)),
            dma,
        ],
        compiler_params=pltpu.CompilerParams(
            collective_id=1, has_side_effects=True, vmem_limit_bytes=VMEM_BYTES
        ),
        name="scatter",
    )(grads, probe_sum)


def solution(mesh):
    return jax.shard_map(
        shards,
        mesh=mesh,
        in_specs=(
            P("probe", None, None, None),
            P("depth", "probe", None, None, None),
            P("depth", None, None),
            P("depth", None, None),
            P(),
            P("probe", None),
        ),
        out_specs=(P("depth", None, "probe", None), P(None, "probe", "depth")),
        check_vma=False,
    )
```
